32 devices in a mesh: groups: 2 (over x), tok: 16 (over z, y, core).
Axes of the slice: x: 2, y: 2, z: 4, core: 2. Of those that a mesh axis runs over, the one named last changes fastest.
Arguments:
- queries: bfloat16 [2, 8192, 1024], P(None, ('groups', 'tok')), parts along dimension 1, may hold values from -6 to 6
- keys: bfloat16 [2, 8192, 1024], P(None, ('groups', 'tok')), parts along dimension 1, may hold values from -6 to 6
- values: bfloat16 [2, 8192, 1024], P(None, ('groups', 'tok')), parts along dimension 1, may hold values from -6 to 6
- rates: float32 [2, 3, 2, 8192], P(None, None, None, ('groups', 'tok')), parts along dimension 3, may hold values from 0.0002 to 0.002
- fast_weights: float32 [2, 3, 512, 512], P(None, None, 'tok'), may hold values from -0.25 to 0.25
Outputs:
- attended: bfloat16 [2, 8192, 1024], P(None, ('groups', 'tok')), parts along dimension 1
- final_weights: float32 [4, 3, 512, 512], P('groups', None, 'tok'), parts along dimension 0
The draws below stay inside these ranges and needn't reach their ends.
There are 2 independent parts, one for each index of `groups`. The reference program is written for one: setup_inputs(seed, part) draws one part's arguments, and reference() takes and returns one part's arrays. A program takes and returns all parts, laid end to end along the dimension named above; an argument that names none is the same for every part. Nothing has to cross between parts.
All inputs are finite; a program needn't handle non-finite values.
Results may differ from the reference program's by a relative error of at most 0.0098.
Values may be sent and summed in bfloat16 or wider, within the bound.
A program may use at most 64 MiB of HBM per device.

```python
import math
import jax
import jax.numpy as jnp
from jax import lax

H = 2
DH = 512
HID = 512
NCHUNK = 2
SPAN = 4096
WIDTH = 1024


def level_of(key, extent, cuts, least, largest):
    loudness = 1.0
    for position, parts in cuts:
        draws = jax.random.uniform(jax.random.fold_in(jax.random.fold_in(key, 6), position), (parts,), jnp.float32, least / len(cuts), largest / len(cuts))
        loudness = loudness * jnp.repeat(jnp.exp(draws), extent[position] // parts).reshape((-1,) + (1,) * (len(extent) - 1 - position))
    return loudness


def bell_draw(own_key, shape, spread, bound, shards=(), held_as=jnp.bfloat16):
    array = jax.random.normal(own_key, shape, jnp.float32) * spread
    if len(shards) > 0:
        array = level_of(own_key, shape, shards, -0.22, 0.18) * array
    return jnp.clip(array, min=-bound, max=bound).astype(held_as)


def setup_inputs(seed: int = 0, part: int = 0) -> dict:
    key_list = jax.random.split(jax.random.key(seed), 6)
    own_keys = jax.random.split(jax.random.fold_in(key_list[5], part), 6)
    queries = bell_draw(own_keys[0], (NCHUNK, SPAN, WIDTH), 1.0, 6.0, ((1, 16),))
    keys = bell_draw(own_keys[1], (NCHUNK, SPAN, WIDTH), 1.0, 6.0, ((1, 16),))
    values = bell_draw(own_keys[2], (NCHUNK, SPAN, WIDTH), 1.0, 6.0, ((1, 16),))
    rates = jnp.clip(jnp.exp(math.log(0.002) - 2.3025852 * jax.random.uniform(own_keys[3], (NCHUNK, 3, H, SPAN), jnp.float32) ** level_of(own_keys[3], (NCHUNK, 3, H, SPAN), ((3, 16),), -0.2, 0.2)), 0.0002, 0.002)
    fast_weights = bell_draw(key_list[4], (H, 3, HID, DH), DH ** -0.5, 0.25, ((2, 16),), jnp.float32)
    return dict(queries=queries, keys=keys, values=values, rates=rates, fast_weights=fast_weights)


def cross(left, right):
    return lax.dot_general(left, right, (((1,), (1,)), ((), ())), preferred_element_type=jnp.float32)

def inner(left, right):
    return lax.dot_general(left, right, (((0,), (0,)), ((), ())), preferred_element_type=jnp.float32)

def renorm(old, upd):
    old_norm = jnp.sqrt(lax.optimization_barrier(jnp.mean(old * old, axis=-1)))
    new_norm = jnp.sqrt(lax.optimization_barrier(jnp.mean(upd * upd, axis=-1)) + 1e-06)
    return upd * (old_norm / new_norm)[..., None]

def head_step(query, key_rows, value_rows, rate_rows, wbf):
    hidden_q = (jax.nn.silu(cross(query, wbf[0])) * cross(query, wbf[1])).astype(jnp.bfloat16)
    raw = cross(hidden_q, wbf[2])
    normed = (raw / jnp.sqrt(lax.optimization_barrier(jnp.mean(raw * raw, axis=-1, keepdims=True)) + 1e-06)).astype(jnp.bfloat16)
    h1 = cross(key_rows, wbf[0])
    h3 = cross(key_rows, wbf[1])
    sig = jax.nn.sigmoid(h1)
    act = h1 * sig
    back = jnp.dot(value_rows, wbf[2], preferred_element_type=jnp.float32)
    d1 = back * h3 * sig * (1.0 + h1 * (1.0 - sig))
    d3 = back * act
    e1 = (rate_rows[0][:, None] * d1).astype(jnp.bfloat16)
    e3 = (rate_rows[1][:, None] * d3).astype(jnp.bfloat16)
    b2 = (rate_rows[2][:, None] * (act * h3)).astype(jnp.bfloat16)
    grad = jnp.stack([inner(e1, key_rows), inner(e3, key_rows), inner(value_rows, b2)])
    return (normed, grad)

def reference(queries, keys, values, rates, fast_weights):
    weights = fast_weights
    blocks = []
    for span in range(NCHUNK):
        wbf = weights.astype(jnp.bfloat16)
        pieces = []
        grads = []
        for head in range(H):
            lo = head * DH
            normed, grad = head_step(queries[span][:, lo:lo + DH], keys[span][:, lo:lo + DH], values[span][:, lo:lo + DH], rates[span][:, head], wbf[head])
            pieces.append(normed)
            grads.append(grad)
        blocks.append(jnp.concatenate(pieces, axis=1))
        weights = renorm(weights, weights + jnp.stack(grads))
    return (jnp.stack(blocks), weights)
```

```python
import functools
import jax
import jax.numpy as jnp
from jax import lax
from jax.experimental import pallas as pl
from jax.experimental.pallas import tpu as pltpu
from jax.sharding import PartitionSpec as P

F32 = jnp.float32
BF16 = jnp.bfloat16


def cross(left, right):
    return lax.dot_general(left, right, (((1,), (1,)), ((), ())), preferred_element_type=F32)


def inner(left, right):
    return lax.dot_general(left, right, (((0,), (0,)), ((), ())), preferred_element_type=F32)


def renorm(old, upd):
    old_norm = jnp.sqrt(jnp.mean(old * old, axis=-1, keepdims=True))
    new_norm = jnp.sqrt(jnp.mean(upd * upd, axis=-1, keepdims=True) + 1e-06)
    return upd * (old_norm / new_norm)


def head_step(query, key_rows, value_rows, rate_rows, wbf):
    hidden_q = (jax.nn.silu(cross(query, wbf[0])) * cross(query, wbf[1])).astype(BF16)
    raw = cross(hidden_q, wbf[2])
    normed = (raw / jnp.sqrt(jnp.mean(raw * raw, axis=-1, keepdims=True) + 1e-06)).astype(BF16)
    h1 = cross(key_rows, wbf[0])
    h3 = cross(key_rows, wbf[1])
    sig = jax.nn.sigmoid(h1)
    act = h1 * sig
    back = jnp.dot(value_rows, wbf[2], preferred_element_type=F32)
    d1 = back * h3 * sig * (1.0 + h1 * (1.0 - sig))
    d3 = back * act
    e1 = (rate_rows[0][:, None] * d1).astype(BF16)
    e3 = (rate_rows[1][:, None] * d3).astype(BF16)
    b2 = (rate_rows[2][:, None] * (act * h3)).astype(BF16)
    grad = jnp.stack([inner(e1, key_rows), inner(e3, key_rows), inner(value_rows, b2)])
    return (normed, grad)


def plain_on_device(queries, keys, values, rates, fast_weights):
    own = fast_weights
    heads, _, _, width = own.shape
    blocks = []
    for span in range(queries.shape[0]):
        gathered = lax.all_gather(own.astype(BF16), "tok", axis=2, tiled=True)
        pieces, grads = [], []
        for head in range(heads):
            cols = slice(head * width, (head + 1) * width)
            normed, grad = head_step(
                queries[span][:, cols],
                keys[span][:, cols],
                values[span][:, cols],
                rates[span][:, head],
                gathered[head],
            )
            pieces.append(normed)
            grads.append(grad)
        blocks.append(jnp.concatenate(pieces, axis=1))
        total = lax.psum_scatter(jnp.stack(grads), "tok", scatter_dimension=2, tiled=True)
        own = renorm(own, own + total)
    return (jnp.stack(blocks), own)


def merge(*gens):
    gens = list(gens)
    while gens:
        for gen in list(gens):
            try:
                next(gen)
            except StopIteration:
                gens.remove(gen)


def kernel(
    nz, ny,
    q_hbm, k_hbm, v_hbm, rates_ref, w_ref,
    out_ref, fin_ref,
    q_ref, k_ref, v_ref, vt_ref, cur, wg, part, sibrecv, ysend, yrecv, zsend, zrecv, acc,
    in_sem, ag_ssem, ag_rsem, sib_ssem, sib_rsem, y_ssem, y_rsem, z_ssem, z_rsem,
):
    spans, tokens, _ = q_ref.shape
    heads, _, rows, dh = w_ref.shape
    tok = 2 * nz * ny
    units = nz * ny
    hid = tok * rows

    me = lax.axis_index("tok")
    c = lax.rem(me, 2)
    y = lax.rem(me // 2, ny)
    z = me // (2 * ny)
    up = me + 2 * ny
    down = me - 2 * ny
    across = me + 2 * (1 - 2 * y)
    sib = me + 1 - 2 * c

    def at(zz, yy, cc):
        return (zz * ny + yy) * 2 + cc

    def rdma(src, dst, ssem, rsem, dev):
        return pltpu.make_async_remote_copy(
            src_ref=src, dst_ref=dst, send_sem=ssem, recv_sem=rsem,
            device_id={"tok": dev}, device_id_type=pl.DeviceIdType.MESH,
        )

    loads = [
        pltpu.make_async_copy(src, dst, in_sem.at[i])
        for i, (src, dst) in enumerate(((k_hbm, k_ref), (v_hbm, v_ref), (q_hbm, q_ref)))
    ]
    for load in loads:
        load.start()

    barrier = pltpu.get_barrier_semaphore()

    def greet(dev):
        pl.semaphore_signal(
            barrier, inc=1, device_id={"tok": dev}, device_id_type=pl.DeviceIdType.MESH
        )

    pl.when(z < nz - 1)(lambda: greet(up))
    pl.when(z > 0)(lambda: greet(down))
    if ny > 1:
        greet(across)
    greet(sib)
    for h in range(heads):
        cur[h] = w_ref[h]
        wg[0, h, me] = w_ref[h].astype(BF16)
    pl.semaphore_wait(
        barrier,
        jnp.where(z < nz - 1, 1, 0) + jnp.where(z > 0, 1, 0) + (2 if ny > 1 else 1),
    )

    def ag_copy(s, h, slot, way):
        dev = (up, down, across, sib)[way]
        ref = wg.at[s, h, slot]
        return rdma(ref, ref, ag_ssem.at[s, h, way, slot], ag_rsem.at[s, h, slot], dev)

    def ag_start(s, h):
        pl.when(z < nz - 1)(lambda: ag_copy(s, h, me, 0).start())
        pl.when(z > 0)(lambda: ag_copy(s, h, me, 1).start())
        if ny > 1:
            ag_copy(s, h, me, 2).start()
        ag_copy(s, h, me, 3).start()

    def ag_steps(s, h):
        def from_z(slot, way):
            ag_copy(s, h, slot, way).wait_recv()
            pl.when((z < nz - 1) if way == 0 else (z > 0))(
                lambda: ag_copy(s, h, slot, way).start()
            )
            if ny > 1:
                ag_copy(s, h, slot, 2).start()
            ag_copy(s, h, slot, 3).start()

        def from_y(slot):
            ag_copy(s, h, slot, 3).wait_recv()
            ag_copy(s, h, slot, 3).start()

        for j in range(1, nz + 1):
            if j < nz:
                pl.when(z - j >= 0)(lambda: from_z(at(z - j, y, c), 0))
                pl.when(z + j < nz)(lambda: from_z(at(z + j, y, c), 1))
            if ny > 1:
                d = j - 1
                if d == 0:
                    from_y(at(z, 1 - y, c))
                else:
                    pl.when(z - d >= 0)(lambda: from_y(at(z - d, 1 - y, c)))
                    pl.when(z + d < nz)(lambda: from_y(at(z + d, 1 - y, c)))
            yield
        for u in range(units):
            ag_copy(s, h, u * 2 + 1 - c, 3).wait_recv()

    def ag_drain(s, h):
        for zz in range(nz):
            slot = at(zz, y, c)
            pl.when((zz <= z) & (z < nz - 1))(lambda: ag_copy(s, h, slot, 0).wait_send())
            pl.when((zz >= z) & (z > 0))(lambda: ag_copy(s, h, slot, 1).wait_send())
            if ny > 1:
                ag_copy(s, h, slot, 2).wait_send()
            for yy in range(ny):
                ag_copy(s, h, at(zz, yy, c), 3).wait_send()

    def weight(s, h, m):
        return wg[s, h, :, m].reshape(hid, dh)

    def cols(h):
        return slice(h * dh, (h + 1) * dh)

    def sib_copy(s, h, m):
        return rdma(
            part.at[s, h, m, 1 - c], sibrecv.at[s, h, m],
            sib_ssem.at[s, h, m], sib_rsem.at[s, h, m], sib,
        )

    def give(s, h, m, grad):
        grad = grad.astype(BF16).reshape(units, 2, rows, dh)
        part[s, h, m, 0] = grad[:, 0]
        part[s, h, m, 1] = grad[:, 1]
        sib_copy(s, h, m).start()

    def kv_steps(s, h):
        key = k_ref[s, :, cols(h)]
        h1 = cross(weight(s, h, 0), key)
        h3 = cross(weight(s, h, 1), key)
        yield
        back = inner(weight(s, h, 2), vt_ref[s, h])
        sig = 1.0 / (1.0 + jnp.exp(-h1))
        act = h1 * sig
        b2 = (rates_ref[s, 2, h : h + 1, :] * (act * h3)).astype(BF16)
        give(s, h, 2, cross(vt_ref[s, h], b2))
        yield
        e1 = (
            rates_ref[s, 0, h : h + 1, :] * (back * h3 * sig * (1.0 + h1 * (1.0 - sig)))
        ).astype(BF16)
        give(s, h, 0, jnp.dot(e1, key, preferred_element_type=F32))
        yield
        e3 = (rates_ref[s, 1, h : h + 1, :] * (back * act)).astype(BF16)
        give(s, h, 1, jnp.dot(e3, key, preferred_element_type=F32))
        yield

    def q_steps(s, h):
        query = q_ref[s, :, cols(h)]
        h1 = cross(query, weight(s, h, 0))
        h3 = cross(query, weight(s, h, 1))
        hidden = (h1 / (1.0 + jnp.exp(-h1)) * h3).astype(BF16)
        yield
        raw = cross(hidden, weight(s, h, 2))
        scale = lax.rsqrt(jnp.mean(raw * raw, axis=-1, keepdims=True) + 1e-06)
        out_ref[s, :, cols(h)] = (raw * scale).astype(BF16)
        yield

    def y_copy(s, h, zd):
        return rdma(
            ysend.at[s, h, zd], yrecv.at[s, h, zd],
            y_ssem.at[s, h, zd], y_rsem.at[s, h, zd], across,
        )

    def z_copy(s, h, zd, way):
        return rdma(
            zsend.at[s, h, zd], zrecv.at[s, h, way, zd],
            z_ssem.at[s, h, zd], z_rsem.at[s, h, way, zd], (up, down)[way],
        )

    def pair(s, h, m, u):
        return part[s, h, m, c, u].astype(F32) + sibrecv[s, h, m, u].astype(F32)

    def rs_steps(s, h):
        for m in (2, 0, 1):
            sib_copy(s, h, m).wait_recv()

        def send_y(zd):
            for m in range(3):
                ysend[s, h, zd, m] = pair(s, h, m, zd * ny + 1 - y).astype(BF16)
            y_copy(s, h, zd).start()

        if ny > 1:
            for d in range(nz - 1, 0, -1):
                pl.when(z + d < nz)(lambda: send_y(z + d))
                pl.when(z - d >= 0)(lambda: send_y(z - d))
            send_y(z)
        yield

        def quad(zd, m):
            value = pair(s, h, m, zd * ny + y)
            if ny > 1:
                value = value + yrecv[s, h, zd, m].astype(F32)
            return value

        def send_z(zd, way):
            more = (z > 0) if way == 0 else (z < nz - 1)
            if ny > 1:
                y_copy(s, h, zd).wait_recv()

            @pl.when(more)
            def _():
                z_copy(s, h, zd, way).wait_recv()
                for m in range(3):
                    zsend[s, h, zd, m] = (
                        quad(zd, m) + zrecv[s, h, way, zd, m].astype(F32)
                    ).astype(BF16)

            @pl.when(jnp.logical_not(more))
            def _():
                for m in range(3):
                    zsend[s, h, zd, m] = quad(zd, m).astype(BF16)

            z_copy(s, h, zd, way).start()

        for d in range(nz - 1, 0, -1):
            pl.when(z + d < nz)(lambda: send_z(z + d, 0))
            pl.when(z - d >= 0)(lambda: send_z(z - d, 1))
            yield
        if ny > 1:
            y_copy(s, h, z).wait_recv()
        for m in range(3):
            acc[m] = quad(z, m)

        def add(way):
            z_copy(s, h, z, way).wait_recv()
            for m in range(3):
                acc[m] = acc[m] + zrecv[s, h, way, z, m].astype(F32)

        pl.when(z > 0)(lambda: add(0))
        pl.when(z < nz - 1)(lambda: add(1))
        old = cur[h]
        new = renorm(old, old + acc[...])
        if s + 1 < spans:
            cur[h] = new
            wg[s + 1, h, me] = new.astype(BF16)
            ag_start(s + 1, h)
        else:
            fin_ref[h] = new

    def rs_drain(s, h):
        for m in range(3):
            sib_copy(s, h, m).wait_send()
        for zd in range(nz):
            if ny > 1:
                y_copy(s, h, zd).wait_send()
            pl.when(zd > z)(lambda: z_copy(s, h, zd, 0).wait_send())
            pl.when(zd < z)(lambda: z_copy(s, h, zd, 1).wait_send())

    def then(*gens):
        for gen in gens:
            yield from gen

    for h in range(heads):
        ag_start(0, h)
    loads[0].wait()
    loads[1].wait()
    for s in range(spans):
        for h in range(heads):
            vt_ref[s, h] = v_ref[s, :, cols(h)].T
    loads[2].wait()

    for s in range(spans):
        if s == 0:
            merge(ag_steps(s, 0))
        for h in range(heads):
            others = []
            if h + 1 < heads:
                others.append(ag_steps(s, h + 1))
            if h > 0:
                others.append(rs_steps(s, h - 1))
            merge(kv_steps(s, h), *others)
        last = [rs_steps(s, heads - 1)]
        if s + 1 < spans:
            last.append(ag_steps(s + 1, 0))
        merge(then(*[q_steps(s, h) for h in range(heads)]), *last)
    for s in range(spans):
        for h in range(heads):
            ag_drain(s, h)
            rs_drain(s, h)


def fused_on_device(nz, ny, queries, keys, values, rates, fast_weights):
    spans, tokens, width = queries.shape
    heads, three, rows, dh = fast_weights.shape
    tok = 2 * nz * ny
    units = nz * ny
    unit = (three, rows, dh)
    sh = (spans, heads)
    vmem = pl.BlockSpec(memory_space=pltpu.VMEM)
    hbm = pl.BlockSpec(memory_space=pl.ANY)
    dma = pltpu.SemaphoreType.DMA
    flops = 18 * spans * heads * tokens * dh * tok * rows
    return pl.pallas_call(
        functools.partial(kernel, nz, ny),
        out_shape=(
            jax.ShapeDtypeStruct(queries.shape, BF16),
            jax.ShapeDtypeStruct(fast_weights.shape, F32),
        ),
        in_specs=[hbm, hbm, hbm, vmem, vmem],
        out_specs=(vmem, vmem),
        scratch_shapes=[
            pltpu.VMEM(queries.shape, BF16),
            pltpu.VMEM(queries.shape, BF16),
            pltpu.VMEM(queries.shape, BF16),
            pltpu.VMEM(sh + (dh, tokens), BF16),
            pltpu.VMEM(fast_weights.shape, F32),
            pltpu.VMEM(sh + (tok,) + unit, BF16),
            pltpu.VMEM(sh + (three, 2, units, rows, dh), BF16),
            pltpu.VMEM(sh + (three, units, rows, dh), BF16),
            pltpu.VMEM(sh + (nz,) + unit, BF16),
            pltpu.VMEM(sh + (nz,) + unit, BF16),
            pltpu.VMEM(sh + (nz,) + unit, BF16),
            pltpu.VMEM(sh + (2, nz) + unit, BF16),
            pltpu.VMEM(unit, F32),
            dma((3,)),
            dma(sh + (4, tok)),
            dma(sh + (tok,)),
            dma(sh + (three,)),
            dma(sh + (three,)),
            dma(sh + (nz,)),
            dma(sh + (nz,)),
            dma(sh + (nz,)),
            dma(sh + (2, nz)),
        ],
        compiler_params=pltpu.CompilerParams(
            collective_id=0, has_side_effects=True, vmem_limit_bytes=56 * 1024 * 1024
        ),
        cost_estimate=pl.CostEstimate(
            flops=flops, bytes_accessed=8 * queries.size, transcendentals=0
        ),
    )(queries, keys, values, rates, fast_weights)


def solution(mesh):
    placed = (
        P(None, ("groups", "tok"), None),
        P(None, ("groups", "tok"), None),
        P(None, ("groups", "tok"), None),
        P(None, None, None, ("groups", "tok")),
        P(None, None, "tok", None),
    )
    tok = mesh.shape["tok"]

    def on_device(queries, keys, values, rates, fast_weights):
        rows = fast_weights.shape[2]
        if rows % 16 or tok % 4:
            return plain_on_device(queries, keys, values, rates, fast_weights)
        return fused_on_device(tok // 4, 2, queries, keys, values, rates, fast_weights)

    return jax.shard_map(
        on_device,
        mesh=mesh,
        in_specs=placed,
        out_specs=(P(None, ("groups", "tok"), None), P("groups", None, "tok", None)),
        check_vma=False,
    )
```

```python
import functools
import jax
import jax.numpy as jnp
from jax import lax
from jax.experimental import pallas as pl
from jax.experimental.pallas import tpu as pltpu
from jax.sharding import PartitionSpec as P

F32 = jnp.float32
BF16 = jnp.bfloat16


def cross(left, right):
    return lax.dot_general(left, right, (((1,), (1,)), ((), ())), preferred_element_type=F32)


def inner(left, right):
    return lax.dot_general(left, right, (((0,), (0,)), ((), ())), preferred_element_type=F32)


def renorm(old, upd):
    old_norm = jnp.sqrt(jnp.mean(old * old, axis=-1, keepdims=True))
    new_norm = jnp.sqrt(jnp.mean(upd * upd, axis=-1, keepdims=True) + 1e-06)
    return upd * (old_norm / new_norm)


def head_step(query, key_rows, value_rows, rate_rows, wbf):
    hidden_q = (jax.nn.silu(cross(query, wbf[0])) * cross(query, wbf[1])).astype(BF16)
    raw = cross(hidden_q, wbf[2])
    normed = (raw / jnp.sqrt(jnp.mean(raw * raw, axis=-1, keepdims=True) + 1e-06)).astype(BF16)
    h1 = cross(key_rows, wbf[0])
    h3 = cross(key_rows, wbf[1])
    sig = jax.nn.sigmoid(h1)
    act = h1 * sig
    back = jnp.dot(value_rows, wbf[2], preferred_element_type=F32)
    d1 = back * h3 * sig * (1.0 + h1 * (1.0 - sig))
    d3 = back * act
    e1 = (rate_rows[0][:, None] * d1).astype(BF16)
    e3 = (rate_rows[1][:, None] * d3).astype(BF16)
    b2 = (rate_rows[2][:, None] * (act * h3)).astype(BF16)
    grad = jnp.stack([inner(e1, key_rows), inner(e3, key_rows), inner(value_rows, b2)])
    return (normed, grad)


def plain_on_device(queries, keys, values, rates, fast_weights):
    own = fast_weights
    heads, _, _, width = own.shape
    blocks = []
    for span in range(queries.shape[0]):
        gathered = lax.all_gather(own.astype(BF16), "tok", axis=2, tiled=True)
        pieces, grads = [], []
        for head in range(heads):
            cols = slice(head * width, (head + 1) * width)
            normed, grad = head_step(
                queries[span][:, cols],
                keys[span][:, cols],
                values[span][:, cols],
                rates[span][:, head],
                gathered[head],
            )
            pieces.append(normed)
            grads.append(grad)
        blocks.append(jnp.concatenate(pieces, axis=1))
        total = lax.psum_scatter(jnp.stack(grads), "tok", scatter_dimension=2, tiled=True)
        own = renorm(own, own + total)
    return (jnp.stack(blocks), own)


HOP = 3.0
GAP = 8.0
FLOW = 8.0
WORK = 0.9
GROUPS = ((0, 1, 2),)


def kernel(
    nz, ny,
    q_hbm, k_hbm, v_hbm, rates_ref, w_ref,
    out_ref, fin_ref,
    q_ref, k_ref, v_ref, vt_ref, cur, wg, part, sibrecv, ysend, yrecv, zsend, zrecv, acc,
    in_sem, ag_ssem, ag_rsem, sib_ssem, sib_rsem, y_ssem, y_rsem, z_ssem, z_rsem,
):
    spans, tokens, _ = q_ref.shape
    heads, _, rows, dh = w_ref.shape
    tok = 2 * nz * ny
    units = nz * ny
    hid = tok * rows
    pieces = [(h, ms) for h in range(heads) for ms in GROUPS]
    gather_order = [
        p for h in range(heads)
        for p in sorted(
            (p for p in range(len(pieces)) if pieces[p][0] == h), key=lambda p: pieces[p][1]
        )
    ]

    me = lax.axis_index("tok")
    c = lax.rem(me, 2)
    y = lax.rem(me // 2, ny)
    z = me // (2 * ny)
    up = me + 2 * ny
    down = me - 2 * ny
    across = me + 2 * (1 - 2 * y)
    sib = me + 1 - 2 * c

    def at(zz, yy, cc):
        return (zz * ny + yy) * 2 + cc

    def rdma(src, dst, ssem, rsem, dev):
        return pltpu.make_async_remote_copy(
            src_ref=src, dst_ref=dst, send_sem=ssem, recv_sem=rsem,
            device_id={"tok": dev}, device_id_type=pl.DeviceIdType.MESH,
        )

    loads = [
        pltpu.make_async_copy(src, dst, in_sem.at[i])
        for i, (src, dst) in enumerate(((k_hbm, k_ref), (v_hbm, v_ref), (q_hbm, q_ref)))
    ]
    for load in loads:
        load.start()

    barrier = pltpu.get_barrier_semaphore()

    def greet(dev):
        pl.semaphore_signal(
            barrier, inc=1, device_id={"tok": dev}, device_id_type=pl.DeviceIdType.MESH
        )

    pl.when(z < nz - 1)(lambda: greet(up))
    pl.when(z > 0)(lambda: greet(down))
    if ny > 1:
        greet(across)
    greet(sib)
    for h in range(heads):
        cur[h] = w_ref[h]
        wg[0, h, me] = w_ref[h].astype(BF16)
    pl.semaphore_wait(
        barrier,
        jnp.where(z < nz - 1, 1, 0) + jnp.where(z > 0, 1, 0) + (2 if ny > 1 else 1),
    )

    def ag_copy(s, p, slot, way):
        dev = (up, down, across, sib)[way]
        h, ms = pieces[p]
        ref = wg.at[s, h, slot, pl.ds(ms[0], len(ms))]
        return rdma(ref, ref, ag_ssem.at[s, p, way, slot], ag_rsem.at[s, p, slot], dev)

    def ag_start(s, p):
        pl.when(z < nz - 1)(lambda: ag_copy(s, p, me, 0).start())
        pl.when(z > 0)(lambda: ag_copy(s, p, me, 1).start())
        if ny > 1:
            ag_copy(s, p, me, 2).start()
        ag_copy(s, p, me, 3).start()

    def ag_steps(s, p):
        def from_z(slot, way):
            ag_copy(s, p, slot, way).wait_recv()
            pl.when((z < nz - 1) if way == 0 else (z > 0))(
                lambda: ag_copy(s, p, slot, way).start()
            )
            if ny > 1:
                ag_copy(s, p, slot, 2).start()
            ag_copy(s, p, slot, 3).start()

        def from_y(slot):
            ag_copy(s, p, slot, 3).wait_recv()
            ag_copy(s, p, slot, 3).start()

        for j in range(1, nz + 1):
            if j < nz:
                pl.when(z - j >= 0)(lambda: from_z(at(z - j, y, c), 0))
                pl.when(z + j < nz)(lambda: from_z(at(z + j, y, c), 1))
            if ny > 1:
                d = j - 1
                if d == 0:
                    from_y(at(z, 1 - y, c))
                else:
                    pl.when(z - d >= 0)(lambda: from_y(at(z - d, 1 - y, c)))
                    pl.when(z + d < nz)(lambda: from_y(at(z + d, 1 - y, c)))
            yield
        for u in range(units):
            ag_copy(s, p, u * 2 + 1 - c, 3).wait_recv()

    def ag_drain(s, p):
        for zz in range(nz):
            slot = at(zz, y, c)
            pl.when((zz <= z) & (z < nz - 1))(lambda: ag_copy(s, p, slot, 0).wait_send())
            pl.when((zz >= z) & (z > 0))(lambda: ag_copy(s, p, slot, 1).wait_send())
            if ny > 1:
                ag_copy(s, p, slot, 2).wait_send()
            for yy in range(ny):
                ag_copy(s, p, at(zz, yy, c), 3).wait_send()

    def weight(s, h, m):
        return wg[s, h, :, m].reshape(hid, dh)

    def cols(h):
        return slice(h * dh, (h + 1) * dh)

    def sib_copy(s, h, m):
        return rdma(
            part.at[s, h, m, 1 - c], sibrecv.at[s, h, m],
            sib_ssem.at[s, h, m], sib_rsem.at[s, h, m], sib,
        )

    def give(s, h, m, grad):
        grad = grad.astype(BF16).reshape(units, 2, rows, dh)
        part[s, h, m, 0] = grad[:, 0]
        part[s, h, m, 1] = grad[:, 1]
        sib_copy(s, h, m).start()

    def kv_steps(s, h):
        key = k_ref[s, :, cols(h)]
        h1 = cross(weight(s, h, 0), key)
        h3 = cross(weight(s, h, 1), key)
        yield
        back = inner(weight(s, h, 2), vt_ref[s, h])
        sig = 1.0 / (1.0 + jnp.exp(-h1))
        act = h1 * sig
        b2 = (rates_ref[s, 2, h : h + 1, :] * (act * h3)).astype(BF16)
        give(s, h, 2, cross(vt_ref[s, h], b2))
        yield
        e1 = (
            rates_ref[s, 0, h : h + 1, :] * (back * h3 * sig * (1.0 + h1 * (1.0 - sig)))
        ).astype(BF16)
        give(s, h, 0, jnp.dot(e1, key, preferred_element_type=F32))
        yield
        e3 = (rates_ref[s, 1, h : h + 1, :] * (back * act)).astype(BF16)
        give(s, h, 1, jnp.dot(e3, key, preferred_element_type=F32))
        yield

    def q_steps(s, h):
        query = q_ref[s, :, cols(h)]
        h1 = cross(query, weight(s, h, 0))
        h3 = cross(query, weight(s, h, 1))
        hidden = (h1 / (1.0 + jnp.exp(-h1)) * h3).astype(BF16)
        yield
        raw = cross(hidden, weight(s, h, 2))
        scale = lax.rsqrt(jnp.mean(raw * raw, axis=-1, keepdims=True) + 1e-06)
        out_ref[s, :, cols(h)] = (raw * scale).astype(BF16)
        yield

    def y_copy(s, p, zd):
        h, ms = pieces[p]
        part_of = pl.ds(ms[0], len(ms))
        return rdma(
            ysend.at[s, h, zd, part_of], yrecv.at[s, h, zd, part_of],
            y_ssem.at[s, p, zd], y_rsem.at[s, p, zd], across,
        )

    def z_copy(s, p, zd, way):
        h, ms = pieces[p]
        part_of = pl.ds(ms[0], len(ms))
        return rdma(
            zsend.at[s, h, zd, part_of], zrecv.at[s, h, way, zd, part_of],
            z_ssem.at[s, p, zd], z_rsem.at[s, p, way, zd], (up, down)[way],
        )

    def pair(s, h, m, u):
        return part[s, h, m, c, u].astype(F32) + sibrecv[s, h, m, u].astype(F32)

    def rs_steps(s, p):
        h, ms = pieces[p]
        for m in ms:
            sib_copy(s, h, m).wait_recv()

        def send_y(zd):
            for m in ms:
                ysend[s, h, zd, m] = pair(s, h, m, zd * ny + 1 - y).astype(BF16)
            y_copy(s, p, zd).start()

        if ny > 1:
            for d in range(nz - 1, 0, -1):
                pl.when(z + d < nz)(lambda: send_y(z + d))
                pl.when(z - d >= 0)(lambda: send_y(z - d))
            send_y(z)
        yield

        def quad(zd, m):
            value = pair(s, h, m, zd * ny + y)
            if ny > 1:
                value = value + yrecv[s, h, zd, m].astype(F32)
            return value

        def send_z(zd, way):
            more = (z > 0) if way == 0 else (z < nz - 1)
            if ny > 1:
                y_copy(s, p, zd).wait_recv()

            @pl.when(more)
            def _():
                z_copy(s, p, zd, way).wait_recv()
                for m in ms:
                    zsend[s, h, zd, m] = (
                        quad(zd, m) + zrecv[s, h, way, zd, m].astype(F32)
                    ).astype(BF16)

            @pl.when(jnp.logical_not(more))
            def _():
                for m in ms:
                    zsend[s, h, zd, m] = quad(zd, m).astype(BF16)

            z_copy(s, p, zd, way).start()

        for d in range(nz - 1, 0, -1):
            pl.when(z + d < nz)(lambda: send_z(z + d, 0))
            pl.when(z - d >= 0)(lambda: send_z(z - d, 1))
            yield
        if ny > 1:
            y_copy(s, p, z).wait_recv()
        for m in ms:
            acc[m] = quad(z, m)

        def add(way):
            z_copy(s, p, z, way).wait_recv()
            for m in ms:
                acc[m] = acc[m] + zrecv[s, h, way, z, m].astype(F32)

        pl.when(z > 0)(lambda: add(0))
        pl.when(z < nz - 1)(lambda: add(1))
        for m in ms:
            old = cur[h, m]
            new = renorm(old, old + acc[m])
            if s + 1 < spans:
                cur[h, m] = new
                wg[s + 1, h, me, m] = new.astype(BF16)
            else:
                fin_ref[h, m] = new
        if s + 1 < spans:
            ag_start(s + 1, p)
        yield

    def rs_drain(s, p):
        h, ms = pieces[p]
        for m in ms:
            sib_copy(s, h, m).wait_send()
        for zd in range(nz):
            if ny > 1:
                y_copy(s, p, zd).wait_send()
            pl.when(zd > z)(lambda: z_copy(s, p, zd, 0).wait_send())
            pl.when(zd < z)(lambda: z_copy(s, p, zd, 1).wait_send())

    for p in gather_order:
        ag_start(0, p)
    loads[0].wait()
    loads[1].wait()
    for s in range(spans):
        for h in range(heads):
            vt_ref[s, h] = v_ref[s, :, cols(h)].T
    loads[2].wait()

    tasks = []

    def plan(gen, times):
        for time in times:
            tasks.append((time, len(tasks), gen))
        return times[-1]

    def until(start, end=0.0):
        return [start + HOP * j for j in range(1, nz + 1)] + [start + HOP * nz + 1.0 + end]

    ready = {}
    for i, p in enumerate(gather_order):
        ready[p] = plan(ag_steps(0, p), until(GAP * i))
    busy = 0.0
    for s in range(spans):
        link = 0.0
        fresh = {}
        for h in range(heads):
            own = [p for p in range(len(pieces)) if pieces[p][0] == h]
            begin = max(busy, max(ready[p] for p in own)) + 0.1
            stages = [begin + WORK * j for j in range(4)]
            busy = plan(kv_steps(s, h), stages)
            for p in own:
                given = max(stages[{2: 1, 0: 2, 1: 3}[m]] for m in pieces[p][1])
                link = max(given + 1.5, link)
                rs = [link] + [link + HOP * j for j in range(1, nz + 1)]
                end = plan(rs_steps(s, p), rs)
                if s + 1 < spans:
                    fresh[p] = plan(ag_steps(s + 1, p), until(end))
                link += FLOW if s + 1 < spans else GAP
        for h in range(heads):
            start = busy + 1.6 + h * 4.0
            plan(q_steps(s, h), [start, start + 2.0])
        ready = fresh
    for _, _, gen in sorted(tasks, key=lambda task: task[:2]):
        next(gen, None)
    for s in range(spans):
        for p in range(len(pieces)):
            ag_drain(s, p)
            rs_drain(s, p)


def fused_on_device(nz, ny, queries, keys, values, rates, fast_weights):
    spans, tokens, width = queries.shape
    heads, three, rows, dh = fast_weights.shape
    tok = 2 * nz * ny
    units = nz * ny
    unit = (three, rows, dh)
    sh = (spans, heads)
    sp = (spans, heads * len(GROUPS))
    vmem = pl.BlockSpec(memory_space=pltpu.VMEM)
    hbm = pl.BlockSpec(memory_space=pl.ANY)
    dma = pltpu.SemaphoreType.DMA
    flops = 18 * spans * heads * tokens * dh * tok * rows
    return pl.pallas_call(
        functools.partial(kernel, nz, ny),
        out_shape=(
            jax.ShapeDtypeStruct(queries.shape, BF16),
            jax.ShapeDtypeStruct(fast_weights.shape, F32),
        ),
        in_specs=[hbm, hbm, hbm, vmem, vmem],
        out_specs=(vmem, vmem),
        scratch_shapes=[
            pltpu.VMEM(queries.shape, BF16),
            pltpu.VMEM(queries.shape, BF16),
            pltpu.VMEM(queries.shape, BF16),
            pltpu.VMEM(sh + (dh, tokens), BF16),
            pltpu.VMEM(fast_weights.shape, F32),
            pltpu.VMEM(sh + (tok,) + unit, BF16),
            pltpu.VMEM(sh + (three, 2, units, rows, dh), BF16),
            pltpu.VMEM(sh + (three, units, rows, dh), BF16),
            pltpu.VMEM(sh + (nz,) + unit, BF16),
            pltpu.VMEM(sh + (nz,) + unit, BF16),
            pltpu.VMEM(sh + (nz,) + unit, BF16),
            pltpu.VMEM(sh + (2, nz) + unit, BF16),
            pltpu.VMEM(unit, F32),
            dma((3,)),
            dma(sp + (4, tok)),
            dma(sp + (tok,)),
            dma(sh + (three,)),
            dma(sh + (three,)),
            dma(sp + (nz,)),
            dma(sp + (nz,)),
            dma(sp + (nz,)),
            dma(sp + (2, nz)),
        ],
        compiler_params=pltpu.CompilerParams(
            collective_id=0, has_side_effects=True, vmem_limit_bytes=56 * 1024 * 1024
        ),
        cost_estimate=pl.CostEstimate(
            flops=flops, bytes_accessed=8 * queries.size, transcendentals=0
        ),
    )(queries, keys, values, rates, fast_weights)


def solution(mesh):
    placed = (
        P(None, ("groups", "tok"), None),
        P(None, ("groups", "tok"), None),
        P(None, ("groups", "tok"), None),
        P(None, None, None, ("groups", "tok")),
        P(None, None, "tok", None),
    )
    tok = mesh.shape["tok"]

    def on_device(queries, keys, values, rates, fast_weights):
        rows = fast_weights.shape[2]
        if rows % 16 or tok % 4:
            return plain_on_device(queries, keys, values, rates, fast_weights)
        return fused_on_device(tok // 4, 2, queries, keys, values, rates, fast_weights)

    return jax.shard_map(
        on_device,
        mesh=mesh,
        in_specs=placed,
        out_specs=(P(None, ("groups", "tok"), None), P("groups", None, "tok", None)),
        check_vma=False,
    )
```
